1024 devices in a mesh: wide: 64 (over y, x, core), narrow: 16 (over z).
Axes of the slice: x: 4, y: 8, z: 16, core: 2. Of those that a mesh axis runs over, the one named last changes fastest.
Arguments:
- tokens: bfloat16 [4096, 4096], P('wide', 'narrow'), may hold values from -6 to 6
- cotangent: bfloat16 [4096, 4096], P('wide', 'narrow'), may hold values from -6 to 6
- expert_ids: int32 [4096, 1], P('wide'), may hold values from 0 to 63; in each aligned block of 64 rows (0 to 63, 64 to 127, ...) at most 2 rows name the same one
- gate_weight: bfloat16 [64, 4096, 2048], P('wide', None, 'narrow'), may hold values from -0.125 to 0.125
- up_weight: bfloat16 [64, 4096, 2048], P('wide', None, 'narrow'), may hold values from -0.125 to 0.125
- down_weight: bfloat16 [64, 2048, 4096], P('wide', 'narrow'), may hold values from -0.1875 to 0.1875
Outputs:
- mixed: bfloat16 [4096, 4096], P('wide', 'narrow')
- grad_tokens: bfloat16 [4096, 4096], P('wide', 'narrow')
The draws below stay inside these ranges and needn't reach their ends.
Inputs may be any that keep to these rules, and one draw needn't show every extreme that they name: `expert_ids`: within each group of 64 consecutive tokens no expert is named by more than 2 tokens, and in some group an expert is named by exactly 2. Every expert is named by some token.
All inputs are finite; a program needn't handle non-finite values.
Results may differ from the reference program's by a relative error of at most 0.024.
Values may be sent and summed in bfloat16 or wider, within the bound.
A program may use at most 32 MiB of HBM per device.

```python
import math
import jax
import jax.numpy as jnp
import numpy as np
from jax import lax

D = 4096
FF = 2048
CAP = 2
EXPERTS = 64
TOK_GRP = 64
TOKENS = 4096
FF_DEV = 128
N_WIDE = 64
N_NARROW = 16


def strengthened(entries, own_key, source, target, blocks, factor):
    owner, partner = [(jnp.arange(entries.shape[dim]) // (entries.shape[dim] // blocks)).reshape([-1 if axis == dim else 1 for axis in range(entries.ndim)]) for dim in (source, target)]
    chosen = jax.random.permutation(own_key, blocks)[partner]
    strong = (owner == chosen) | (owner == (partner + blocks // 2) % blocks)
    return jnp.where(strong, factor * entries, entries)


def shard_levels(key, extent, shards, least, high):
    loudness, own = 1.0, jax.random.fold_in(key, 6)
    for dim, blocks in shards:
        heights = jnp.exp(jax.random.uniform(jax.random.fold_in(own, dim), (blocks,), jnp.float32, least / len(shards), high / len(shards)))
        loudness = loudness * jnp.repeat(heights, extent[dim] // blocks).reshape([-1 if axis == dim else 1 for axis in range(len(extent))])
    return loudness


def deal_out(own_key, own, number, rows, number_of, top, most, skew):
    sequence = jax.random.permutation(own_key, number_of)
    crowded, ordinary = load_shares(number_of, rows * top, most, skew, True), load_shares(number_of, rows * top, most, skew, False)
    places = jnp.arange(number_of)

    def named(tallies, offset_by):
        used = int((tallies > 0).sum())
        fixed = max(1, used // 4)
        passed = fixed + (places - fixed + offset_by * (used - fixed)) % max(1, number_of - fixed)
        return jnp.zeros((number_of,), jnp.int32).at[sequence[jnp.where(places < fixed, places, passed)]].set(jnp.asarray(tallies, jnp.int32))

    tallies = jnp.where(number % 4 == 0, named(crowded, number // 4), named(ordinary, number - number // 4 - 1))
    mixed = jax.random.permutation(jax.random.fold_in(own, 3), number_of)
    source_of, receiver = mixed[0:number_of // 2 * 2:2], mixed[1:number_of // 2 * 2:2]
    margin = jnp.minimum(tallies[source_of] - 1, most - tallies[receiver]) // 2
    margin = jnp.where((source_of == sequence[0]) | (receiver == sequence[0]) | (tallies[receiver] == 0), 0, jnp.maximum(margin, 0))
    passed = jax.random.randint(jax.random.fold_in(own, 4), (number_of // 2,), 0, 1 << 20) % (margin + 1)
    tallies = tallies.at[source_of].add(-passed).at[receiver].add(passed)
    labels = jnp.searchsorted(jnp.cumsum(tallies), jnp.arange(rows * top), side="right").astype(jnp.int32)
    grid = labels.reshape(top, rows).T
    grid = grid[jax.random.permutation(jax.random.fold_in(own, 1), rows)]
    offset_by = jax.random.randint(jax.random.fold_in(own, 2), (rows, 1), 0, top)
    return jnp.take_along_axis(grid, (jnp.arange(top)[None, :] + offset_by) % top, axis=1)


def load_shares(amount, total, reach, lean, full):
    portions = [(1 << 20) // math.isqrt(grade ** lean) + 1 for grade in range(1, amount + 1)]
    largest = reach if full else min(reach, max(-(-total // amount), total * portions[0] // sum(portions)))
    least = 1 if total - largest >= amount - 1 else 0
    given, rest = [largest] + [least] * (amount - 1), total - largest - least * (amount - 1)
    while rest > 0:
        free = [i for i in range(1, amount) if given[i] < largest] or [i for i in range(1, amount) if given[i] < reach]
        whole, remaining = sum([portions[i] for i in free]), rest
        for i in free:
            more = min(reach - given[i], max(1, remaining * portions[i] // whole), rest)
            given[i] = given[i] + more
            rest = rest - more
    return np.array(given)


def gaussian(own_key, extent, width, limit, split=(), kind=jnp.bfloat16):
    loudness = shard_levels(own_key, extent, split, -0.22, 0.18) if split else 1.0
    entries = jax.random.normal(own_key, extent, jnp.float32) * width * loudness
    return jnp.minimum(jnp.maximum(entries, -limit), limit).astype(kind)


def gaussian_with(own_key, extent, scale, reach, pieces, heavy, kind=jnp.bfloat16):
    result = scale * jax.random.normal(own_key, extent, jnp.float32)
    if pieces:
        result = result * shard_levels(own_key, extent, pieces, -0.22, 0.18)
    return jnp.clip(strengthened(result, jax.random.fold_in(own_key, 3), *heavy), -reach, reach).astype(kind)


def setup_inputs(seed: int = 0) -> dict:
    key_list = jax.random.split(jax.random.key(seed), 7)
    tokens = gaussian(key_list[0], (TOKENS, D), 1.0, 6.0, ((0, 64), (1, 16)))
    cotangent = gaussian(key_list[1], (TOKENS, D), 1.0, 6.0, ((0, 64), (1, 16)))
    expert_ids_keys = jax.random.split(jax.random.fold_in(key_list[2], 1), TOKENS // TOK_GRP)
    expert_ids_turns = jax.random.permutation(jax.random.fold_in(key_list[2], 3), TOKENS // TOK_GRP)
    expert_ids = jax.vmap(lambda own, number: deal_out(jax.random.fold_in(key_list[2], 2), own, number, TOK_GRP, EXPERTS, 1, CAP, 2))(expert_ids_keys, expert_ids_turns).reshape((TOKENS, 1))
    gate_weight = gaussian_with(key_list[3], (EXPERTS, D, FF), D ** -0.5, 0.125, ((0, 64), (2, 16)), (2, 1, 16, 2.0))
    up_weight = gaussian_with(key_list[4], (EXPERTS, D, FF), D ** -0.5, 0.125, ((0, 64), (2, 16)), (2, 1, 16, 2.0))
    down_weight = gaussian_with(key_list[5], (EXPERTS, FF, D), FF ** -0.5, 0.1875, ((0, 64), (1, 16)), (1, 2, 16, 2.0))
    return dict(tokens=tokens, cotangent=cotangent, expert_ids=expert_ids, gate_weight=gate_weight, up_weight=up_weight, down_weight=down_weight)


def block_sums(parts):
    rounded = lax.optimization_barrier(parts.astype(jnp.bfloat16))
    return jnp.sum(rounded.astype(jnp.float32), axis=0).astype(jnp.bfloat16)


def reference(tokens, cotangent, expert_ids, gate_weight, up_weight, down_weight):
    ids = expert_ids[:, 0].reshape(N_WIDE, TOK_GRP)
    onehot = (ids[:, :, None] == jnp.arange(EXPERTS, dtype=jnp.int32)[None, None, :]).astype(jnp.int32)
    before = jnp.cumsum(onehot, axis=1) - onehot
    slot = jnp.sum(before * onehot, axis=2)
    target = ids * CAP + slot
    placing = (jnp.arange(EXPERTS * CAP, dtype=jnp.int32)[None, :, None] == target[:, None, :]).astype(jnp.bfloat16)
    tok = tokens.reshape(N_WIDE, TOK_GRP, D)
    cot = cotangent.reshape(N_WIDE, TOK_GRP, D)

    def spread(pair):
        return jnp.dot(pair[0], pair[1], preferred_element_type=jnp.float32).astype(jnp.bfloat16)

    def to_experts(buffer):
        return buffer.reshape(N_WIDE, EXPERTS, CAP, D).transpose(1, 0, 2, 3).reshape(EXPERTS, N_WIDE * CAP, D)

    buf_tok = to_experts(lax.map(spread, (placing, tok)))
    buf_cot = to_experts(lax.map(spread, (placing, cot)))

    def expert(items):
        rows, cots, w_gate, w_up, w_down = items
        gate = jnp.dot(rows, w_gate, preferred_element_type=jnp.float32)
        up = jnp.dot(rows, w_up, preferred_element_type=jnp.float32)
        sig = jax.nn.sigmoid(gate)
        hidden = (gate * sig * up).astype(jnp.bfloat16)
        count = rows.shape[0]
        down_f = w_down.astype(jnp.float32).reshape(N_NARROW, FF_DEV, D)
        hid_f = hidden.astype(jnp.float32).reshape(count, N_NARROW, FF_DEV)
        out = block_sums(jnp.einsum('rnf,nfd->nrd', hid_f, down_f))
        back = lax.dot_general(cots, w_down, (((1,), (1,)), ((), ())), preferred_element_type=jnp.float32)
        d_gate = (back * up * sig * (1.0 + gate * (1.0 - sig))).astype(jnp.bfloat16)
        d_up = (back * gate * sig).astype(jnp.bfloat16)
        gate_f = w_gate.astype(jnp.float32).reshape(D, N_NARROW, FF_DEV)
        up_f = w_up.astype(jnp.float32).reshape(D, N_NARROW, FF_DEV)
        dg_f = d_gate.astype(jnp.float32).reshape(count, N_NARROW, FF_DEV)
        du_f = d_up.astype(jnp.float32).reshape(count, N_NARROW, FF_DEV)
        parts = jnp.einsum('rnf,dnf->nrd', dg_f, gate_f) + jnp.einsum('rnf,dnf->nrd', du_f, up_f)
        return out, block_sums(parts)

    outs, grads = lax.map(expert, (buf_tok, buf_cot, gate_weight, up_weight, down_weight))

    def to_groups(buffer):
        return buffer.reshape(EXPERTS, N_WIDE, CAP, D).transpose(1, 0, 2, 3).reshape(N_WIDE, EXPERTS * CAP, D)

    def collect(pair):
        return lax.dot_general(pair[0], pair[1], (((0,), (0,)), ((), ())), preferred_element_type=jnp.float32).astype(jnp.bfloat16)

    mixed = lax.map(collect, (placing, to_groups(outs))).reshape(TOKENS, D)
    grad_tokens = lax.map(collect, (placing, to_groups(grads))).reshape(TOKENS, D)
    return mixed, grad_tokens
```

```python
import functools

import jax
import jax.numpy as jnp
from jax import lax
from jax.experimental import pallas as pl
from jax.experimental.pallas import tpu as pltpu
from jax.sharding import PartitionSpec as P

CAP = 2
INNER = 8
CHUNKS = 2
MESH = pl.DeviceIdType.MESH
F32 = jnp.float32
BF16 = jnp.bfloat16
NT = (((1,), (1,)), ((), ()))


def log2(value):
    return value.bit_length() - 1


def kernel(
    outer, inner, ring, chunks,
    ids_ref, tok_ref, cot_ref, gate_ref, up_ref, down_ref, mixed_ref, gtok_ref,
    ids_v, raw, gu, dn, st1, rx1, st2, gat, gu_acc, back_acc, hid, dgu,
    sbuf, rbuf, bk1, bx1, bk2, bx2, outv,
    in_sem, w_sem, out_sem, a_send, a_recv, g_send, g_recv, r_send, r_recv,
):
    slots = outer * inner * CAP
    group, width = raw.shape[1:]
    ff = hid.shape[1]
    part = slots // chunks
    wide = lax.axis_index("wide")
    me = lax.axis_index("narrow")
    my_o = wide // inner
    my_i = lax.rem(wide, inner)
    right = (wide, lax.rem(me + 1, ring))
    left = (wide, lax.rem(me + ring - 1, ring))

    first = [
        pltpu.make_async_copy(ids_ref, ids_v, in_sem.at[0]),
        pltpu.make_async_copy(tok_ref, raw.at[0], in_sem.at[1]),
        pltpu.make_async_copy(cot_ref, raw.at[1], in_sem.at[2]),
    ]
    weights = [
        pltpu.make_async_copy(gate_ref.at[0], gu.at[:, pl.ds(0, ff)], w_sem.at[0]),
        pltpu.make_async_copy(up_ref.at[0], gu.at[:, pl.ds(ff, ff)], w_sem.at[1]),
        pltpu.make_async_copy(down_ref.at[0], dn, w_sem.at[2]),
    ]
    for copy in first + weights:
        copy.start()

    outer_peers = [lax.rem(my_o + k, outer) for k in range(1, outer)]
    inner_peers = [lax.rem(my_i + k, inner) for k in range(1, inner)]
    peers = [(o * inner + my_i, me) for o in outer_peers]
    peers += [(my_o * inner + i, me) for i in inner_peers]
    peers += [right, left]
    barrier = pltpu.get_barrier_semaphore()
    for peer in peers:
        pl.semaphore_signal(barrier, inc=1, device_id=peer, device_id_type=MESH)

    for copy in first:
        copy.wait()
    ids_row = jnp.broadcast_to(ids_v[...].astype(F32), (group, group))
    i0 = lax.broadcasted_iota(jnp.int32, (group, group), 0)
    i1 = lax.broadcasted_iota(jnp.int32, (group, group), 1)
    ids_col = jnp.sum(jnp.where(i0 == i1, ids_row, 0.0), axis=1, keepdims=True)
    same = ids_col == ids_row
    slot_row = jnp.sum(jnp.where(same & (i0 < i1), 1.0, 0.0), axis=0, keepdims=True)
    slot_col = jnp.sum(jnp.where(same & (i1 < i0), 1.0, 0.0), axis=1, keepdims=True)
    target_row = (ids_row[:1] * CAP + slot_row).astype(jnp.int32)
    target_col = (ids_col * CAP + slot_col).astype(jnp.int32)
    spread = (lax.broadcasted_iota(jnp.int32, (slots, group), 0) == target_row).astype(BF16)
    collect = (lax.broadcasted_iota(jnp.int32, (group, slots), 1) == target_col).astype(BF16)
    r0 = lax.broadcasted_iota(jnp.int32, (slots, slots), 0)
    r1 = lax.broadcasted_iota(jnp.int32, (slots, slots), 1)

    def turned(r, low, high):
        cap, a, b = r & (CAP - 1), (r >> 1) & (low - 1), r >> (1 + log2(low))
        return (a * high + b) * CAP + cap

    to_inner = (r1 == turned(r0, outer, inner)).astype(BF16)
    to_outer = (r1 == turned(r0, inner, outer)).astype(BF16)

    pl.semaphore_wait(barrier, len(peers))

    def rows_of(index, count):
        return pl.ds(pl.multiple_of(index * count, count), count)

    def swap(stage, t, src, dst, to_outer_peers):
        count = inner * CAP if to_outer_peers else outer * CAP
        mine = my_o if to_outer_peers else my_i
        targets = outer_peers if to_outer_peers else inner_peers
        for k, p in enumerate(targets):
            device = (p * inner + my_i, me) if to_outer_peers else (my_o * inner + p, me)
            pltpu.make_async_remote_copy(
                src_ref=src.at[rows_of(p, count)],
                dst_ref=dst.at[rows_of(mine, count)],
                send_sem=a_send.at[stage, t],
                recv_sem=a_recv.at[stage, t],
                device_id=device,
                device_id_type=MESH,
            ).start()
        dst[rows_of(mine, count)] = src[rows_of(mine, count)]

    def swap_wait(stage, t, src, dst, to_outer_peers, send):
        count = inner * CAP if to_outer_peers else outer * CAP
        moved = pl.ds(0, slots - count)
        sem = a_send if send else a_recv
        pltpu.make_async_copy(src.at[moved], dst.at[moved], sem.at[stage, t]).wait()

    for t in range(2):
        st1[t] = jnp.dot(spread, raw[t], preferred_element_type=F32).astype(BF16)
        swap(0, t, st1.at[t], rx1.at[t], True)
    for t in range(2):
        swap_wait(0, t, st1.at[t], rx1.at[t], True, False)
        st2[t] = jnp.dot(to_inner, rx1[t], preferred_element_type=F32).astype(BF16)
        swap(1, t, st2.at[t], gat.at[t, me], False)

    def hops(t, d):
        longer = ring // 2
        return longer if t == d else ring - 1 - longer

    def gather_copy(t, d, s, c):
        owner = lax.rem(me + (ring - s if d == 0 else s), ring)
        chunk = gat.at[t, owner, pl.ds(c * part, part)]
        return pltpu.make_async_remote_copy(
            src_ref=chunk, dst_ref=chunk,
            send_sem=g_send.at[t, d, s], recv_sem=g_recv.at[t, d, s, c],
            device_id=right if d == 0 else left, device_id_type=MESH,
        )

    def gather_send(t, d, s):
        for c in range(chunks):
            gather_copy(t, d, s, c).start()

    def gather_sent(t, d, s):
        block = gat.at[t, 0]
        pltpu.make_async_copy(block, block, g_send.at[t, d, s]).wait()

    def use_block(t, owner):
        block = gat[t, owner]
        if t == 0:
            gu_acc[...] += jnp.dot(block, gu[rows_of(owner, width)], preferred_element_type=F32)
        else:
            back_acc[...] += lax.dot_general(
                block, dn[:, rows_of(owner, width)], NT, preferred_element_type=F32
            )

    def gather_step(t, s):
        for c in range(chunks):
            for d in range(2):
                if s < hops(t, d):
                    gather_copy(t, d, s, c).wait_recv()
                    if s + 1 < hops(t, d):
                        gather_copy(t, d, s + 1, c).start()
        for d in range(2):
            if s < hops(t, d):
                use_block(t, lax.rem(me + (ring - 1 - s if d == 0 else 1 + s), ring))
                gather_sent(t, d, s)

    def term(u, dest):
        if u == 0:
            return jnp.dot(hid[...], dn[:, rows_of(dest, width)], preferred_element_type=F32)
        return lax.dot_general(dgu[...], gu[rows_of(dest, width)], NT, preferred_element_type=F32)

    def sum_copy(u, d, s, c):
        chunk = pl.ds(c * part, part)
        return pltpu.make_async_remote_copy(
            src_ref=sbuf.at[u, d, s, chunk], dst_ref=rbuf.at[u, d, s, chunk],
            send_sem=r_send.at[u, d, s], recv_sem=r_recv.at[u, d, s, c],
            device_id=right if d == 0 else left, device_id_type=MESH,
        )

    def sum_step(u, s):
        live = [d for d in range(2) if s < hops(u, d)]
        terms = {}
        for d in live:
            far = hops(u, d) - s
            terms[d] = term(u, lax.rem(me + (far if d == 0 else ring - far), ring))
        for c in range(chunks):
            chunk = pl.ds(c * part, part)
            for d in live:
                value = terms[d][c * part:(c + 1) * part]
                if s > 0:
                    sum_copy(u, d, s - 1, c).wait_recv()
                    value = value + rbuf[u, d, s - 1, chunk].astype(F32)
                sbuf[u, d, s, chunk] = value.astype(BF16)
                sum_copy(u, d, s, c).start()

    def sum_end(u):
        total = term(u, me)
        for c in range(chunks):
            chunk = pl.ds(c * part, part)
            value = total[c * part:(c + 1) * part]
            for d in range(2):
                last = hops(u, d) - 1
                sum_copy(u, d, last, c).wait_recv()
                value = value + rbuf[u, d, last, chunk].astype(F32)
            bk1[u, chunk] = value.astype(BF16)
        swap(2, u, bk1.at[u], bx1.at[u], False)

    def back_turn(u):
        swap_wait(2, u, bk1.at[u], bx1.at[u], False, False)
        bk2[u] = jnp.dot(to_outer, bx1[u], preferred_element_type=F32).astype(BF16)
        swap(3, u, bk2.at[u], bx2.at[u], True)

    def back_end(u):
        swap_wait(3, u, bk2.at[u], bx2.at[u], True, False)
        outv[u] = jnp.dot(collect, bx2[u], preferred_element_type=F32).astype(BF16)
        pltpu.make_async_copy(outv.at[u], (mixed_ref, gtok_ref)[u], out_sem.at[u]).start()

    def sum_sent(u, d, s):
        pltpu.make_async_copy(sbuf.at[u, d, s], rbuf.at[u, d, s], r_send.at[u, d, s]).wait()

    gu_acc[...] = jnp.zeros_like(gu_acc)
    back_acc[...] = jnp.zeros_like(back_acc)
    for t in range(2):
        swap_wait(1, t, st2.at[t], gat.at[t, me], False, False)
        for d in range(2):
            gather_send(t, d, 0)
    for copy in weights:
        copy.wait()
    for t in range(2):
        use_block(t, me)
        swap_wait(0, t, st1.at[t], rx1.at[t], True, True)
        swap_wait(1, t, st2.at[t], gat.at[t, me], False, True)

    longest = ring // 2
    for s in range(longest):
        gather_step(0, s)
    gate = gu_acc[:, :ff]
    up = gu_acc[:, ff:]
    sig = jax.nn.sigmoid(gate)
    hid[...] = (gate * sig * up).astype(BF16)
    sum_step(0, 0)
    for s in range(longest):
        gather_step(1, s)
    gate = gu_acc[:, :ff]
    up = gu_acc[:, ff:]
    sig = jax.nn.sigmoid(gate)
    back = back_acc[...]
    dgu[:, :ff] = (back * up * sig * (1.0 + gate * (1.0 - sig))).astype(BF16)
    dgu[:, ff:] = (back * gate * sig).astype(BF16)
    sum_step(1, 0)
    for s in range(1, longest):
        sum_step(0, s)
    sum_end(0)
    for s in range(1, longest):
        sum_step(1, s)
        if s == longest // 3:
            back_turn(0)
        if s == 2 * longest // 3:
            back_end(0)
    sum_end(1)
    for u in range(2):
        for d in range(2):
            for s in range(hops(u, d)):
                sum_sent(u, d, s)
        swap_wait(2, 0, bk1.at[0], bx1.at[0], False, True) if u == 0 else None
    back_turn(1)
    swap_wait(3, 0, bk2.at[0], bx2.at[0], True, True)
    swap_wait(2, 1, bk1.at[1], bx1.at[1], False, True)
    back_end(1)
    swap_wait(3, 1, bk2.at[1], bx2.at[1], True, True)
    for u in range(2):
        pltpu.make_async_copy(outv.at[u], (mixed_ref, gtok_ref)[u], out_sem.at[u]).wait()


def per_device(inner, tokens, cotangent, expert_ids, gate_weight, up_weight, down_weight):
    groups, ring = lax.axis_size("wide"), lax.axis_size("narrow")
    outer = groups // inner
    slots = groups * CAP
    group, width = tokens.shape
    d_model, ff = gate_weight.shape[1:]
    longest = ring // 2
    out = jax.ShapeDtypeStruct((group, width), BF16)
    any_spec = pl.BlockSpec(memory_space=pl.ANY)
    block = (slots, width)
    dma = pltpu.SemaphoreType.DMA
    return pl.pallas_call(
        functools.partial(kernel, outer, inner, ring, CHUNKS),
        out_shape=(out, out),
        in_specs=[any_spec] * 6,
        out_specs=(any_spec, any_spec),
        scratch_shapes=[
            pltpu.VMEM((1, group), jnp.int32),
            pltpu.VMEM((2, group, width), BF16),
            pltpu.VMEM((d_model, 2 * ff), BF16),
            pltpu.VMEM((ff, d_model), BF16),
            pltpu.VMEM((2,) + block, BF16),
            pltpu.VMEM((2,) + block, BF16),
            pltpu.VMEM((2,) + block, BF16),
            pltpu.VMEM((2, ring) + block, BF16),
            pltpu.VMEM((slots, 2 * ff), F32),
            pltpu.VMEM((slots, ff), F32),
            pltpu.VMEM((slots, ff), BF16),
            pltpu.VMEM((slots, 2 * ff), BF16),
            pltpu.VMEM((2, 2, longest) + block, BF16),
            pltpu.VMEM((2, 2, longest) + block, BF16),
            pltpu.VMEM((2,) + block, BF16),
            pltpu.VMEM((2,) + block, BF16),
            pltpu.VMEM((2,) + block, BF16),
            pltpu.VMEM((2,) + block, BF16),
            pltpu.VMEM((2, group, width), BF16),
            dma((3,)),
            dma((3,)),
            dma((2,)),
            dma((4, 2)),
            dma((4, 2)),
            dma((2, 2, longest)),
            dma((2, 2, longest, CHUNKS)),
            dma((2, 2, longest)),
            dma((2, 2, longest, CHUNKS)),
        ],
        compiler_params=pltpu.CompilerParams(
            collective_id=0, has_side_effects=True, vmem_limit_bytes=40 * 1024 * 1024
        ),
        cost_estimate=pl.CostEstimate(
            flops=12 * slots * d_model * ff, bytes_accessed=6 * d_model * ff, transcendentals=slots * ff
        ),
    )(expert_ids.reshape(1, group), tokens, cotangent, gate_weight, up_weight, down_weight)


def solution(mesh):
    placed = (
        P("wide", "narrow"),
        P("wide", "narrow"),
        P("wide", None),
        P("wide", None, "narrow"),
        P("wide", None, "narrow"),
        P("wide", "narrow", None),
    )
    return jax.shard_map(
        functools.partial(per_device, INNER),
        mesh=mesh,
        in_specs=placed,
        out_specs=(P("wide", "narrow"), P("wide", "narrow")),
        check_vma=False,
    )
```

```python
import functools

import jax
import jax.numpy as jnp
from jax import lax
from jax.experimental import pallas as pl
from jax.experimental.pallas import tpu as pltpu
from jax.sharding import PartitionSpec as P

CAP = 2
INNER = 8
CHUNKS = 2
MESH = pl.DeviceIdType.MESH
F32 = jnp.float32
BF16 = jnp.bfloat16
NT = (((1,), (1,)), ((), ()))


def log2(value):
    return value.bit_length() - 1


def kernel(
    outer, inner, ring, chunks,
    ids_ref, tok_ref, cot_ref, gate_ref, up_ref, down_ref, mixed_ref, gtok_ref,
    ids_v, raw, gu, dn, st1, rx1, st2, gat, gu_acc, back_acc, hid, dgu,
    terms, sbuf, rbuf, bk1, bx1, bk2, bx2, outv,
    in_sem, w_sem, out_sem, a_send, a_recv, g_send, g_recv, r_send, r_recv,
):
    slots = outer * inner * CAP
    group, width = raw.shape[1:]
    ff = hid.shape[1]
    part = slots // chunks
    wide = lax.axis_index("wide")
    me = lax.axis_index("narrow")
    my_o = wide // inner
    my_i = lax.rem(wide, inner)
    right = (wide, lax.rem(me + 1, ring))
    left = (wide, lax.rem(me + ring - 1, ring))

    first = [
        pltpu.make_async_copy(ids_ref, ids_v, in_sem.at[0]),
        pltpu.make_async_copy(tok_ref, raw.at[0], in_sem.at[1]),
        pltpu.make_async_copy(cot_ref, raw.at[1], in_sem.at[2]),
    ]
    weights = [
        pltpu.make_async_copy(gate_ref.at[0], gu.at[:, pl.ds(0, ff)], w_sem.at[0]),
        pltpu.make_async_copy(up_ref.at[0], gu.at[:, pl.ds(ff, ff)], w_sem.at[1]),
        pltpu.make_async_copy(down_ref.at[0], dn, w_sem.at[2]),
    ]
    for copy in first + weights:
        copy.start()

    outer_peers = [lax.rem(my_o + k, outer) for k in range(1, outer)]
    inner_peers = [lax.rem(my_i + k, inner) for k in range(1, inner)]
    peers = [(o * inner + my_i, me) for o in outer_peers]
    peers += [(my_o * inner + i, me) for i in inner_peers]
    peers += [right, left]
    barrier = pltpu.get_barrier_semaphore()
    for peer in peers:
        pl.semaphore_signal(barrier, inc=1, device_id=peer, device_id_type=MESH)

    for copy in first:
        copy.wait()
    ids_row = jnp.broadcast_to(ids_v[...].astype(F32), (group, group))
    i0 = lax.broadcasted_iota(jnp.int32, (group, group), 0)
    i1 = lax.broadcasted_iota(jnp.int32, (group, group), 1)
    ids_col = jnp.sum(jnp.where(i0 == i1, ids_row, 0.0), axis=1, keepdims=True)
    same = ids_col == ids_row
    slot_row = jnp.sum(jnp.where(same & (i0 < i1), 1.0, 0.0), axis=0, keepdims=True)
    slot_col = jnp.sum(jnp.where(same & (i1 < i0), 1.0, 0.0), axis=1, keepdims=True)
    target_row = (ids_row[:1] * CAP + slot_row).astype(jnp.int32)
    target_col = (ids_col * CAP + slot_col).astype(jnp.int32)
    spread = (lax.broadcasted_iota(jnp.int32, (slots, group), 0) == target_row).astype(BF16)
    collect = (lax.broadcasted_iota(jnp.int32, (group, slots), 1) == target_col).astype(BF16)
    r0 = lax.broadcasted_iota(jnp.int32, (slots, slots), 0)
    r1 = lax.broadcasted_iota(jnp.int32, (slots, slots), 1)

    def turned(r, low, high):
        cap, a, b = r & (CAP - 1), (r >> 1) & (low - 1), r >> (1 + log2(low))
        return (a * high + b) * CAP + cap

    to_inner = (r1 == turned(r0, outer, inner)).astype(BF16)
    to_outer = (r1 == turned(r0, inner, outer)).astype(BF16)

    pl.semaphore_wait(barrier, len(peers))

    def rows_of(index, count):
        return pl.ds(pl.multiple_of(index * count, count), count)

    def swap(stage, t, src, dst, to_outer_peers):
        count = inner * CAP if to_outer_peers else outer * CAP
        mine = my_o if to_outer_peers else my_i
        targets = outer_peers if to_outer_peers else inner_peers
        for k, p in enumerate(targets):
            device = (p * inner + my_i, me) if to_outer_peers else (my_o * inner + p, me)
            pltpu.make_async_remote_copy(
                src_ref=src.at[rows_of(p, count)],
                dst_ref=dst.at[rows_of(mine, count)],
                send_sem=a_send.at[stage, t],
                recv_sem=a_recv.at[stage, t],
                device_id=device,
                device_id_type=MESH,
            ).start()
        dst[rows_of(mine, count)] = src[rows_of(mine, count)]

    def swap_wait(stage, t, src, dst, to_outer_peers, send):
        count = inner * CAP if to_outer_peers else outer * CAP
        moved = pl.ds(0, slots - count)
        sem = a_send if send else a_recv
        pltpu.make_async_copy(src.at[moved], dst.at[moved], sem.at[stage, t]).wait()

    for t in range(2):
        st1[t] = jnp.dot(spread, raw[t], preferred_element_type=F32).astype(BF16)
        swap(0, t, st1.at[t], rx1.at[t], True)
    for t in range(2):
        swap_wait(0, t, st1.at[t], rx1.at[t], True, False)
        st2[t] = jnp.dot(to_inner, rx1[t], preferred_element_type=F32).astype(BF16)
        swap(1, t, st2.at[t], gat.at[t, me], False)

    def hops(t, d):
        longer = ring // 2
        return longer if t == d else ring - 1 - longer

    def gather_copy(t, d, s, c):
        owner = lax.rem(me + (ring - s if d == 0 else s), ring)
        chunk = gat.at[t, owner, pl.ds(c * part, part)]
        return pltpu.make_async_remote_copy(
            src_ref=chunk, dst_ref=chunk,
            send_sem=g_send.at[t, d, s], recv_sem=g_recv.at[t, d, s, c],
            device_id=right if d == 0 else left, device_id_type=MESH,
        )

    def gather_send(t, d, s):
        for c in range(chunks):
            gather_copy(t, d, s, c).start()

    def gather_sent(t, d, s):
        block = gat.at[t, 0]
        pltpu.make_async_copy(block, block, g_send.at[t, d, s]).wait()

    def use_block(t, owner):
        block = gat[t, owner]
        if t == 0:
            gu_acc[...] += jnp.dot(block, gu[rows_of(owner, width)], preferred_element_type=F32)
        else:
            back_acc[...] += lax.dot_general(
                block, dn[:, rows_of(owner, width)], NT, preferred_element_type=F32
            )

    def gather_step(s):
        for c in range(chunks):
            for t in range(2):
                for d in range(2):
                    if s < hops(t, d):
                        gather_copy(t, d, s, c).wait_recv()
                        if s + 1 < hops(t, d):
                            gather_copy(t, d, s + 1, c).start()
        for t in range(2):
            for d in range(2):
                if s < hops(t, d):
                    use_block(t, lax.rem(me + (ring - 1 - s if d == 0 else 1 + s), ring))

    def term(u, dest):
        if u == 0:
            return jnp.dot(hid[...], dn[:, rows_of(dest, width)], preferred_element_type=F32)
        return lax.dot_general(dgu[...], gu[rows_of(dest, width)], NT, preferred_element_type=F32)

    def sum_copy(u, d, s, c):
        chunk = pl.ds(c * part, part)
        return pltpu.make_async_remote_copy(
            src_ref=sbuf.at[u, d, s, chunk], dst_ref=rbuf.at[u, d, s, chunk],
            send_sem=r_send.at[u, d, s], recv_sem=r_recv.at[u, d, s, c],
            device_id=right if d == 0 else left, device_id_type=MESH,
        )

    def sum_step(s):
        live = [(u, d) for u in range(2) for d in range(2) if s < hops(u, d)]
        for u, d in live:
            far = hops(u, d) - s
            value = term(u, lax.rem(me + (far if d == 0 else ring - far), ring))
            if s > 0:
                terms[u, d] = value
                continue
            sbuf[u, d, 0] = value.astype(BF16)
            for c in range(chunks):
                sum_copy(u, d, 0, c).start()
        if s == 0:
            return
        for c in range(chunks):
            chunk = pl.ds(c * part, part)
            for u, d in live:
                sum_copy(u, d, s - 1, c).wait_recv()
                value = terms[u, d, chunk] + rbuf[u, d, s - 1, chunk].astype(F32)
                sbuf[u, d, s, chunk] = value.astype(BF16)
                sum_copy(u, d, s, c).start()

    def sum_end(u):
        total = term(u, me)
        for c in range(chunks):
            chunk = pl.ds(c * part, part)
            value = total[c * part:(c + 1) * part]
            for d in range(2):
                last = hops(u, d) - 1
                sum_copy(u, d, last, c).wait_recv()
                value = value + rbuf[u, d, last, chunk].astype(F32)
            bk1[u, chunk] = value.astype(BF16)
        swap(2, u, bk1.at[u], bx1.at[u], False)

    def back_turn(u):
        swap_wait(2, u, bk1.at[u], bx1.at[u], False, False)
        bk2[u] = jnp.dot(to_outer, bx1[u], preferred_element_type=F32).astype(BF16)
        swap(3, u, bk2.at[u], bx2.at[u], True)

    def back_end(u):
        swap_wait(3, u, bk2.at[u], bx2.at[u], True, False)
        outv[u] = jnp.dot(collect, bx2[u], preferred_element_type=F32).astype(BF16)
        pltpu.make_async_copy(outv.at[u], (mixed_ref, gtok_ref)[u], out_sem.at[u]).start()

    def sum_sent(u, d, s):
        pltpu.make_async_copy(sbuf.at[u, d, s], rbuf.at[u, d, s], r_send.at[u, d, s]).wait()

    gu_acc[...] = jnp.zeros_like(gu_acc)
    back_acc[...] = jnp.zeros_like(back_acc)
    for t in range(2):
        swap_wait(1, t, st2.at[t], gat.at[t, me], False, False)
        for d in range(2):
            gather_send(t, d, 0)
    for copy in weights:
        copy.wait()
    for t in range(2):
        use_block(t, me)
        swap_wait(0, t, st1.at[t], rx1.at[t], True, True)
        swap_wait(1, t, st2.at[t], gat.at[t, me], False, True)

    longest = ring // 2
    for s in range(longest):
        gather_step(s)
    gate = gu_acc[:, :ff]
    up = gu_acc[:, ff:]
    sig = jax.nn.sigmoid(gate)
    back = back_acc[...]
    hid[...] = (gate * sig * up).astype(BF16)
    dgu[:, :ff] = (back * up * sig * (1.0 + gate * (1.0 - sig))).astype(BF16)
    dgu[:, ff:] = (back * gate * sig).astype(BF16)
    for s in range(longest):
        sum_step(s)
    for t in range(2):
        for d in range(2):
            for s in range(hops(t, d)):
                gather_sent(t, d, s)
    for u in range(2):
        sum_end(u)
    for u in range(2):
        for d in range(2):
            for s in range(hops(u, d)):
                sum_sent(u, d, s)
    for u in range(2):
        back_turn(u)
    for u in range(2):
        swap_wait(2, u, bk1.at[u], bx1.at[u], False, True)
    for u in range(2):
        back_end(u)
    for u in range(2):
        swap_wait(3, u, bk2.at[u], bx2.at[u], True, True)
    for u in range(2):
        pltpu.make_async_copy(outv.at[u], (mixed_ref, gtok_ref)[u], out_sem.at[u]).wait()


def per_device(inner, tokens, cotangent, expert_ids, gate_weight, up_weight, down_weight):
    groups, ring = lax.axis_size("wide"), lax.axis_size("narrow")
    outer = groups // inner
    slots = groups * CAP
    group, width = tokens.shape
    d_model, ff = gate_weight.shape[1:]
    longest = ring // 2
    out = jax.ShapeDtypeStruct((group, width), BF16)
    any_spec = pl.BlockSpec(memory_space=pltpu.HBM)
    block = (slots, width)
    dma = pltpu.SemaphoreType.DMA
    return pl.pallas_call(
        functools.partial(kernel, outer, inner, ring, CHUNKS),
        out_shape=(out, out),
        in_specs=[any_spec] * 6,
        out_specs=(any_spec, any_spec),
        scratch_shapes=[
            pltpu.VMEM((1, group), jnp.int32),
            pltpu.VMEM((2, group, width), BF16),
            pltpu.VMEM((d_model, 2 * ff), BF16),
            pltpu.VMEM((ff, d_model), BF16),
            pltpu.VMEM((2,) + block, BF16),
            pltpu.VMEM((2,) + block, BF16),
            pltpu.VMEM((2,) + block, BF16),
            pltpu.VMEM((2, ring) + block, BF16),
            pltpu.VMEM((slots, 2 * ff), F32),
            pltpu.VMEM((slots, ff), F32),
            pltpu.VMEM((slots, ff), BF16),
            pltpu.VMEM((slots, 2 * ff), BF16),
            pltpu.VMEM((2, 2) + block, F32),
            pltpu.VMEM((2, 2, longest) + block, BF16),
            pltpu.VMEM((2, 2, longest) + block, BF16),
            pltpu.VMEM((2,) + block, BF16),
            pltpu.VMEM((2,) + block, BF16),
            pltpu.VMEM((2,) + block, BF16),
            pltpu.VMEM((2,) + block, BF16),
            pltpu.VMEM((2, group, width), BF16),
            dma((3,)),
            dma((3,)),
            dma((2,)),
            dma((4, 2)),
            dma((4, 2)),
            dma((2, 2, longest)),
            dma((2, 2, longest, CHUNKS)),
            dma((2, 2, longest)),
            dma((2, 2, longest, CHUNKS)),
        ],
        compiler_params=pltpu.CompilerParams(
            collective_id=0, has_side_effects=True, vmem_limit_bytes=40 * 1024 * 1024
        ),
        cost_estimate=pl.CostEstimate(
            flops=12 * slots * d_model * ff, bytes_accessed=6 * d_model * ff, transcendentals=slots * ff
        ),
    )(expert_ids.reshape(1, group), tokens, cotangent, gate_weight, up_weight, down_weight)


def solution(mesh):
    placed = (
        P("wide", "narrow"),
        P("wide", "narrow"),
        P("wide", None),
        P("wide", None, "narrow"),
        P("wide", None, "narrow"),
        P("wide", "narrow", None),
    )
    return jax.shard_map(
        functools.partial(per_device, INNER),
        mesh=mesh,
        in_specs=placed,
        out_specs=(P("wide", "narrow"), P("wide", "narrow")),
        check_vma=False,
    )
```

```python
import functools

import jax
import jax.numpy as jnp
from jax import lax
from jax.experimental import pallas as pl
from jax.experimental.pallas import tpu as pltpu
from jax.sharding import PartitionSpec as P

CAP = 2
INNER = 8
CHUNKS = 2
VMEM_LIMIT = 63 * 1024 * 1024
MESH = pl.DeviceIdType.MESH
F32 = jnp.float32
BF16 = jnp.bfloat16
NT = (((1,), (1,)), ((), ()))


def log2(value):
    return value.bit_length() - 1


def kernel(
    outer, inner, ring, chunks,
    ids_ref, tok_ref, cot_ref, gate_ref, up_ref, down_ref, mixed_ref, gtok_ref,
    ids_v, raw, gu, dn, st1, rx1, st2, gat, gu_acc, back_acc, hid, dgu,
    terms, sbuf, rbuf, bk1, bx1, bk2, bx2, outv,
    in_sem, w_sem, out_sem, a_send, a_recv, g_send, g_recv, r_send, r_recv,
):
    slots = outer * inner * CAP
    group, width = raw.shape[1:]
    ff = hid.shape[1]
    part = slots // chunks
    wide = lax.axis_index("wide")
    me = lax.axis_index("narrow")
    my_o = wide // inner
    my_i = lax.rem(wide, inner)
    right = (wide, lax.rem(me + 1, ring))
    left = (wide, lax.rem(me + ring - 1, ring))

    first = [
        pltpu.make_async_copy(ids_ref, ids_v, in_sem.at[0]),
        pltpu.make_async_copy(tok_ref, raw.at[0], in_sem.at[1]),
        pltpu.make_async_copy(cot_ref, raw.at[1], in_sem.at[2]),
    ]
    weights = [
        pltpu.make_async_copy(gate_ref.at[0], gu.at[:, pl.ds(0, ff)], w_sem.at[0]),
        pltpu.make_async_copy(up_ref.at[0], gu.at[:, pl.ds(ff, ff)], w_sem.at[1]),
        pltpu.make_async_copy(down_ref.at[0], dn, w_sem.at[2]),
    ]
    for copy in first + weights:
        copy.start()

    outer_peers = [lax.rem(my_o + k, outer) for k in range(1, outer)]
    inner_peers = [lax.rem(my_i + k, inner) for k in range(1, inner)]
    peers = [(o * inner + my_i, me) for o in outer_peers]
    peers += [(my_o * inner + i, me) for i in inner_peers]
    peers += [right, left]
    barrier = pltpu.get_barrier_semaphore()
    for peer in peers:
        pl.semaphore_signal(barrier, inc=1, device_id=peer, device_id_type=MESH)

    for copy in first:
        copy.wait()
    ids_row = jnp.broadcast_to(ids_v[...].astype(F32), (group, group))
    i0 = lax.broadcasted_iota(jnp.int32, (group, group), 0)
    i1 = lax.broadcasted_iota(jnp.int32, (group, group), 1)
    ids_col = jnp.sum(jnp.where(i0 == i1, ids_row, 0.0), axis=1, keepdims=True)
    same = ids_col == ids_row
    slot_row = jnp.sum(jnp.where(same & (i0 < i1), 1.0, 0.0), axis=0, keepdims=True)
    slot_col = jnp.sum(jnp.where(same & (i1 < i0), 1.0, 0.0), axis=1, keepdims=True)
    target_row = (ids_row[:1] * CAP + slot_row).astype(jnp.int32)
    target_col = (ids_col * CAP + slot_col).astype(jnp.int32)
    spread = (lax.broadcasted_iota(jnp.int32, (slots, group), 0) == target_row).astype(BF16)
    collect = (lax.broadcasted_iota(jnp.int32, (group, slots), 1) == target_col).astype(BF16)
    r0 = lax.broadcasted_iota(jnp.int32, (slots, slots), 0)
    r1 = lax.broadcasted_iota(jnp.int32, (slots, slots), 1)

    def turned(r, low, high):
        cap, a, b = r & (CAP - 1), (r >> 1) & (low - 1), r >> (1 + log2(low))
        return (a * high + b) * CAP + cap

    to_inner = (r1 == turned(r0, outer, inner)).astype(BF16)
    to_outer = (r1 == turned(r0, inner, outer)).astype(BF16)

    pl.semaphore_wait(barrier, len(peers))

    def rows_of(index, count):
        return pl.ds(pl.multiple_of(index * count, count), count)

    def swap(stage, t, src, dst, to_outer_peers):
        count = inner * CAP if to_outer_peers else outer * CAP
        mine = my_o if to_outer_peers else my_i
        targets = outer_peers if to_outer_peers else inner_peers
        for k, p in enumerate(targets):
            device = (p * inner + my_i, me) if to_outer_peers else (my_o * inner + p, me)
            pltpu.make_async_remote_copy(
                src_ref=src.at[rows_of(p, count)],
                dst_ref=dst.at[rows_of(mine, count)],
                send_sem=a_send.at[stage, t],
                recv_sem=a_recv.at[stage, t],
                device_id=device,
                device_id_type=MESH,
            ).start()
        dst[rows_of(mine, count)] = src[rows_of(mine, count)]

    def swap_wait(stage, t, src, dst, to_outer_peers, send):
        count = inner * CAP if to_outer_peers else outer * CAP
        moved = pl.ds(0, slots - count)
        sem = a_send if send else a_recv
        pltpu.make_async_copy(src.at[moved], dst.at[moved], sem.at[stage, t]).wait()

    for t in range(2):
        st1[t] = jnp.dot(spread, raw[t], preferred_element_type=F32).astype(BF16)
        swap(0, t, st1.at[t], rx1.at[t], True)
    for t in range(2):
        swap_wait(0, t, st1.at[t], rx1.at[t], True, False)
        st2[t] = jnp.dot(to_inner, rx1[t], preferred_element_type=F32).astype(BF16)
        swap(1, t, st2.at[t], gat.at[t, me], False)

    def hops(t, d):
        longer = ring // 2
        return longer if t == d else ring - 1 - longer

    def gather_copy(t, d, s, c):
        owner = lax.rem(me + (ring - s if d == 0 else s), ring)
        chunk = gat.at[t, owner, pl.ds(c * part, part)]
        return pltpu.make_async_remote_copy(
            src_ref=chunk, dst_ref=chunk,
            send_sem=g_send.at[t, d, s], recv_sem=g_recv.at[t, d, s, c],
            device_id=right if d == 0 else left, device_id_type=MESH,
        )

    def gather_send(t, d, s):
        for c in range(chunks):
            gather_copy(t, d, s, c).start()

    def gather_sent(t, d, s):
        block = gat.at[t, 0]
        pltpu.make_async_copy(block, block, g_send.at[t, d, s]).wait()

    def use_block(t, owner):
        block = gat[t, owner]
        if t == 0:
            gu_acc[...] += jnp.dot(block, gu[rows_of(owner, width)], preferred_element_type=F32)
        else:
            back_acc[...] += lax.dot_general(
                block, dn[:, rows_of(owner, width)], NT, preferred_element_type=F32
            )

    def gather_step(s):
        for c in range(chunks):
            for t in range(2):
                for d in range(2):
                    if s < hops(t, d):
                        gather_copy(t, d, s, c).wait_recv()
                        if s + 1 < hops(t, d):
                            gather_copy(t, d, s + 1, c).start()
        for t in range(2):
            for d in range(2):
                if s < hops(t, d):
                    use_block(t, lax.rem(me + (ring - 1 - s if d == 0 else 1 + s), ring))

    def term(u, dest):
        if u == 0:
            return jnp.dot(hid[...], dn[:, rows_of(dest, width)], preferred_element_type=F32)
        return lax.dot_general(dgu[...], gu[rows_of(dest, width)], NT, preferred_element_type=F32)

    def sum_copy(u, d, s, c):
        chunk = pl.ds(c * part, part)
        return pltpu.make_async_remote_copy(
            src_ref=sbuf.at[u, d, s, chunk], dst_ref=rbuf.at[u, d, s, chunk],
            send_sem=r_send.at[u, d, s], recv_sem=r_recv.at[u, d, s, c],
            device_id=right if d == 0 else left, device_id_type=MESH,
        )

    def sum_step(s):
        live = [(u, d) for u in range(2) for d in range(2) if s < hops(u, d)]
        for u, d in live:
            far = hops(u, d) - s
            value = term(u, lax.rem(me + (far if d == 0 else ring - far), ring))
            if s > 0:
                terms[u, d] = value
                continue
            sbuf[u, d, 0] = value.astype(BF16)
            for c in range(chunks):
                sum_copy(u, d, 0, c).start()
        if s == 0:
            return
        for c in range(chunks):
            chunk = pl.ds(c * part, part)
            for u, d in live:
                sum_copy(u, d, s - 1, c).wait_recv()
                value = terms[u, d, chunk] + rbuf[u, d, s - 1, chunk].astype(F32)
                sbuf[u, d, s, chunk] = value.astype(BF16)
                sum_copy(u, d, s, c).start()

    def sum_end(u):
        total = term(u, me)
        for c in range(chunks):
            chunk = pl.ds(c * part, part)
            value = total[c * part:(c + 1) * part]
            for d in range(2):
                last = hops(u, d) - 1
                sum_copy(u, d, last, c).wait_recv()
                value = value + rbuf[u, d, last, chunk].astype(F32)
            bk1[u, chunk] = value.astype(BF16)
        swap(2, u, bk1.at[u], bx1.at[u], False)

    def back_turn(u):
        swap_wait(2, u, bk1.at[u], bx1.at[u], False, False)
        bk2[u] = jnp.dot(to_outer, bx1[u], preferred_element_type=F32).astype(BF16)
        swap(3, u, bk2.at[u], bx2.at[u], True)

    def back_end(u):
        swap_wait(3, u, bk2.at[u], bx2.at[u], True, False)
        outv[u] = jnp.dot(collect, bx2[u], preferred_element_type=F32).astype(BF16)
        pltpu.make_async_copy(outv.at[u], (mixed_ref, gtok_ref)[u], out_sem.at[u]).start()

    def sum_sent(u, d, s):
        pltpu.make_async_copy(sbuf.at[u, d, s], rbuf.at[u, d, s], r_send.at[u, d, s]).wait()

    gu_acc[...] = jnp.zeros_like(gu_acc)
    back_acc[...] = jnp.zeros_like(back_acc)
    for t in range(2):
        swap_wait(1, t, st2.at[t], gat.at[t, me], False, False)
        for d in range(2):
            gather_send(t, d, 0)
    for copy in weights:
        copy.wait()
    for t in range(2):
        use_block(t, me)
        swap_wait(0, t, st1.at[t], rx1.at[t], True, True)
        swap_wait(1, t, st2.at[t], gat.at[t, me], False, True)

    longest = ring // 2
    for s in range(longest):
        gather_step(s)
    gate = gu_acc[:, :ff]
    up = gu_acc[:, ff:]
    sig = jax.nn.sigmoid(gate)
    back = back_acc[...]
    hid[...] = (gate * sig * up).astype(BF16)
    dgu[:, :ff] = (back * up * sig * (1.0 + gate * (1.0 - sig))).astype(BF16)
    dgu[:, ff:] = (back * gate * sig).astype(BF16)
    for s in range(longest):
        sum_step(s)
        if s < 2:
            for d in range(2):
                for sent in range(hops(s, d)):
                    gather_sent(s, d, sent)
    for u in range(2):
        sum_end(u)
    for u in range(2):
        for d in range(2):
            for s in range(hops(u, d)):
                sum_sent(u, d, s)
    for u in range(2):
        back_turn(u)
    for u in range(2):
        swap_wait(2, u, bk1.at[u], bx1.at[u], False, True)
    for u in range(2):
        back_end(u)
    for u in range(2):
        swap_wait(3, u, bk2.at[u], bx2.at[u], True, True)
    for u in range(2):
        pltpu.make_async_copy(outv.at[u], (mixed_ref, gtok_ref)[u], out_sem.at[u]).wait()


def per_device(inner, tokens, cotangent, expert_ids, gate_weight, up_weight, down_weight):
    groups, ring = lax.axis_size("wide"), lax.axis_size("narrow")
    outer = groups // inner
    slots = groups * CAP
    group, width = tokens.shape
    d_model, ff = gate_weight.shape[1:]
    longest = ring // 2
    out = jax.ShapeDtypeStruct((group, width), BF16)
    any_spec = pl.BlockSpec(memory_space=pltpu.HBM)
    block = (slots, width)
    dma = pltpu.SemaphoreType.DMA
    return pl.pallas_call(
        functools.partial(kernel, outer, inner, ring, CHUNKS),
        out_shape=(out, out),
        in_specs=[any_spec] * 6,
        out_specs=(any_spec, any_spec),
        scratch_shapes=[
            pltpu.VMEM((1, group), jnp.int32),
            pltpu.VMEM((2, group, width), BF16),
            pltpu.VMEM((d_model, 2 * ff), BF16),
            pltpu.VMEM((ff, d_model), BF16),
            pltpu.VMEM((2,) + block, BF16),
            pltpu.VMEM((2,) + block, BF16),
            pltpu.VMEM((2,) + block, BF16),
            pltpu.VMEM((2, ring) + block, BF16),
            pltpu.VMEM((slots, 2 * ff), F32),
            pltpu.VMEM((slots, ff), F32),
            pltpu.VMEM((slots, ff), BF16),
            pltpu.VMEM((slots, 2 * ff), BF16),
            pltpu.VMEM((2, 2) + block, F32),
            pltpu.VMEM((2, 2, longest) + block, BF16),
            pltpu.VMEM((2, 2, longest) + block, BF16),
            pltpu.VMEM((2,) + block, BF16),
            pltpu.VMEM((2,) + block, BF16),
            pltpu.VMEM((2,) + block, BF16),
            pltpu.VMEM((2,) + block, BF16),
            pltpu.VMEM((2, group, width), BF16),
            dma((3,)),
            dma((3,)),
            dma((2,)),
            dma((4, 2)),
            dma((4, 2)),
            dma((2, 2, longest)),
            dma((2, 2, longest, CHUNKS)),
            dma((2, 2, longest)),
            dma((2, 2, longest, CHUNKS)),
        ],
        compiler_params=pltpu.CompilerParams(
            collective_id=0, has_side_effects=True, vmem_limit_bytes=VMEM_LIMIT
        ),
        cost_estimate=pl.CostEstimate(
            flops=12 * slots * d_model * ff, bytes_accessed=6 * d_model * ff, transcendentals=slots * ff
        ),
    )(expert_ids.reshape(1, group), tokens, cotangent, gate_weight, up_weight, down_weight)


def solution(mesh):
    placed = (
        P("wide", "narrow"),
        P("wide", "narrow"),
        P("wide", None),
        P("wide", None, "narrow"),
        P("wide", None, "narrow"),
        P("wide", "narrow", None),
    )
    return jax.shard_map(
        functools.partial(per_device, INNER),
        mesh=mesh,
        in_specs=placed,
        out_specs=(P("wide", "narrow"), P("wide", "narrow")),
        check_vma=False,
    )
```
